256 devices in a mesh: cols: 64 (over x_hi, z, y), rows: 4 (over x_lo, core).
Axes of the slice: x: 4 (x_hi: 2, x_lo: 2; x = x_hi * 2 + x_lo), y: 4, z: 8, core: 2. Of those that a mesh axis runs over, the one named last changes fastest.
Arguments:
- gradient: bfloat16 [8192, 28672], P('rows', 'cols'), may hold values from -6 to 6
- eigenbasis: float32 [8192, 8192], P('rows', 'cols'), may hold values from -0.0625 to 0.0625
- first_moment: float32 [4, 256, 28672], P(None, 'rows', 'cols'), may hold values from -4 to 4
- second_moment: float32 [4, 256, 28672], P(None, 'rows', 'cols'), may hold values from 0.2 to 2
- prior_update: float32 [8192, 28672], P('rows', 'cols'), may hold values from -3 to 3
- group_ids: int32 [4], replicated, may hold values from 0 to 31, as said below
Outputs:
- first_out: float32 [4, 256, 28672], P(None, 'rows', 'cols')
- second_out: float32 [4, 256, 28672], P(None, 'rows', 'cols')
- update: float32 [8192, 28672], P('rows', 'cols')
The draws below stay inside these ranges and needn't reach their ends.
Inputs may be any that keep to these rules, and one draw needn't show every extreme that they name: `group_ids`: the 4 entries are distinct.
All inputs are finite; a program needn't handle non-finite values.
Results may differ from the reference program's by a relative error of at most 0.0003.
Values sent between devices are 32-bit elements; how exact they have to be, the bound alone decides.
A program may use at most 64 MiB of HBM per device.

```python
import math
import jax
import jax.numpy as jnp
from jax import lax

M = 8192
N = 28672
GROUP = 256
GROUPS = 4


def draw_group_ids(key, part):
    blocks = M // GROUP
    inner = jax.random.permutation(jax.random.fold_in(key, 7), blocks - 2) + 1
    chosen = jnp.concatenate([jnp.array([0, blocks - 1], jnp.int32), inner[:GROUPS - 2].astype(jnp.int32)])
    order = jax.random.permutation(jax.random.fold_in(key, 11), GROUPS)
    return chosen[order].astype(jnp.int32)


def levels(rng, extent, shards, low, top_value):
    def one(position, parts):
        draws = jax.random.uniform(jax.random.fold_in(jax.random.fold_in(rng, 6), position), (parts,), jnp.float32, low / len(shards), top_value / len(shards))
        return jnp.repeat(jnp.exp(draws), extent[position] // parts).reshape((-1,) + (1,) * (len(extent) - position - 1))

    level = one(*shards[0])
    for cut in shards[1:]:
        level = level * one(*cut)
    return level


def noise(key, extent, width, limit, shards=(), held_as=jnp.bfloat16):
    gain = levels(key, extent, shards, -0.22, 0.18) if shards else 1.0
    drawn = jax.random.normal(key, extent, jnp.float32) * width * gain
    return jnp.minimum(jnp.maximum(drawn, -limit), limit).astype(held_as)


def setup_inputs(seed: int = 0) -> dict:
    key_list = jax.random.split(jax.random.key(seed), 7)
    gradient = noise(key_list[0], (M, N), 1.0, 6.0, ((0, 4), (1, 64)))
    eigenbasis = noise(key_list[1], (M, M), M ** -0.5, 0.0625, ((0, 4), (1, 64)), jnp.float32)
    first_moment = noise(key_list[2], (GROUPS, GROUP, N), 0.5, 4.0, ((1, 4), (2, 64)), jnp.float32)
    second_moment = jnp.clip(jnp.exp(math.log(2.0) - 2.3025851 * jax.random.uniform(key_list[3], (GROUPS, GROUP, N), jnp.float32) ** levels(key_list[3], (GROUPS, GROUP, N), ((1, 4), (2, 64)), -0.2, 0.2)), 0.2, 2.0)
    prior_update = noise(key_list[4], (M, N), 0.3, 3.0, ((0, 4), (1, 64)), jnp.float32)
    group_ids = draw_group_ids(jax.random.fold_in(key_list[6], 71), 0)
    return {"gradient": gradient, "eigenbasis": eigenbasis, "first_moment": first_moment, "second_moment": second_moment, "prior_update": prior_update, "group_ids": group_ids}


beta_one = 0.9
beta_two = 0.95
correct_one = 1.0 - 0.9 ** 10
correct_two = 1.0 - 0.95 ** 10
epsilon = 1e-08

def reference(gradient, eigenbasis, first_moment, second_moment, prior_update, group_ids):
    grad_float = gradient.astype(jnp.float32)
    update = prior_update
    firsts = []
    seconds = []
    for group_slot in range(GROUPS):
        begin = (group_ids[group_slot] * GROUP).astype(jnp.int32)
        group_basis = lax.dynamic_slice_in_dim(eigenbasis, begin, GROUP, 1)
        rotated = jnp.dot(group_basis.T, grad_float, precision=lax.Precision.HIGHEST, preferred_element_type=jnp.float32)
        moment_one = beta_one * first_moment[group_slot] + (1.0 - beta_one) * rotated
        moment_two = beta_two * second_moment[group_slot] + (1.0 - beta_two) * rotated * rotated
        adjusted = moment_one / correct_one / (jnp.sqrt(moment_two / correct_two) + epsilon)
        update = update + jnp.dot(group_basis, adjusted, precision=lax.Precision.HIGHEST, preferred_element_type=jnp.float32)
        firsts.append(moment_one)
        seconds.append(moment_two)
    return (jnp.stack(firsts), jnp.stack(seconds), update)
```

```python
import functools

import jax
import jax.numpy as jnp
from jax import lax
from jax.experimental import pallas as pl
from jax.experimental.pallas import tpu as pltpu
from jax.sharding import PartitionSpec as P

MESH = pl.DeviceIdType.MESH

GROUPS = 4
NX, NZ, NY = 2, 8, 4
PIECE = 32
GROUP = 256
QUARTER = 64
COLS = 448
ROWS = 2048
SPLIT = (16, 24)

beta_one = 0.9
beta_two = 0.95
correct_one = 1.0 - 0.9**10
correct_two = 1.0 - 0.95**10
epsilon = 1e-08

Z_MSGS = 7
Y_MSGS = 3
Z_TICKS = (0, 1, 2, 3, 4, 5, 6)
Y_BIG_TICKS = (0, 1, 4)
Y_SMALL_TICKS = (0, 1, 2)
TICKS = 8

SEM_X = 0
SEM_A1 = 1
SEM_B1 = SEM_A1 + 2 * Z_MSGS
SEM_A2 = SEM_B1 + 2 * Y_MSGS
SEM_B2 = SEM_A2 + 2 * Y_MSGS
SEM_RS1 = SEM_B2 + 2 * Z_MSGS
SEM_RS2 = SEM_RS1 + 1
SEM_AX = SEM_RS2 + 1
SEM_AC = SEM_AX + 1
SEM_AF = SEM_AC + 1
SEMS = SEM_AF + 1


def split_terms(value):
    high = value.astype(jnp.bfloat16)
    low = (value - high.astype(jnp.float32)).astype(jnp.bfloat16)
    return high, low


def kernel(ids, pieces, first_in, second_in, grad_hbm, prior_hbm,
           first_out, second_out, update_hbm,
           buf, grad, update, partial, rs1, xsend, rs2, adjusted,
           send_sem, recv_sem, local_sem, out_sem):
    cols = lax.axis_index("cols")
    rows = lax.axis_index("rows")
    xh = cols // (NZ * NY)
    z = (cols // NY) % NZ
    y = cols % NY
    xlo = rows // 2
    core = rows % 2
    sign = 1 - 2 * core

    def at(xh_, z_, y_):
        return (xh_ * NZ + z_) * NY + y_

    x_peer = (at(1 - xh, z, y), rows)
    z_peer = {d: (at(xh, (z + d * sign + NZ) % NZ, y), rows) for d in (1, -1)}
    y_peer = {d: (at(xh, z, (y + d * sign + NY) % NY), rows) for d in (1, -1)}
    core_peer = (cols, xlo * 2 + 1 - core)
    chip_peer = (cols, (1 - xlo) * 2 + core)

    grad_copy = pltpu.make_async_copy(grad_hbm, grad, local_sem.at[0])
    prior_copy = pltpu.make_async_copy(prior_hbm, update, local_sem.at[1])
    grad_copy.start()
    prior_copy.start()

    barrier = pltpu.get_barrier_semaphore()
    peers = [x_peer, z_peer[1], z_peer[-1], y_peer[1], y_peer[-1], core_peer, chip_peer]
    for peer in peers:
        pl.semaphore_signal(barrier, inc=1, device_id=peer, device_id_type=MESH)

    for c in range(GROUPS):
        for half in range(2):
            buf[c, xh, z, y, :, half * 128:(half + 1) * 128] = pieces[ids[c] * 2 + half]

    pl.semaphore_wait(barrier, len(peers))

    def remote(src, dst, c, number, peer):
        return pltpu.make_async_remote_copy(
            src_ref=src, dst_ref=dst, send_sem=send_sem.at[c, number], recv_sem=recv_sem.at[c, number],
            device_id=peer, device_id_type=MESH)

    def x_copy(c):
        ref = buf.at[c, xh, z, y]
        return remote(ref, ref, c, SEM_X, x_peer)

    for c in range(GROUPS):
        x_copy(c).start()

    def ring_copy(stream, c, d, i):
        k, h = i // 2, (i % 2 if d == 1 else 1 - i % 2)
        first, second = pl.ds(0, SPLIT[h]), pl.ds(SPLIT[h], PIECE - SPLIT[h])
        zk = (z - d * sign * k + NZ) % NZ
        yk = (y - d * sign * k + 2 * NY) % NY
        lane = 0 if d == 1 else 1
        if stream == "a1":
            ref, number, peer = buf.at[c, h, zk, y, first], SEM_A1 + 2 * i + lane, z_peer[d]
        elif stream == "b1":
            ref, number, peer = buf.at[c, h, z, yk, second], SEM_B1 + 2 * i + lane, y_peer[d]
        elif stream == "a2":
            ref, number, peer = buf.at[c, h, :, yk, first], SEM_A2 + 2 * i + lane, y_peer[d]
        else:
            ref, number, peer = buf.at[c, h, zk, :, second], SEM_B2 + 2 * i + lane, z_peer[d]
        return remote(ref, ref, c, number, peer)

    def run_tick(stream, ticks, c, t):
        if t in ticks:
            i = ticks.index(t)
            for d in (1, -1):
                if i >= 2:
                    ring_copy(stream, c, d, i - 2).wait_recv()
                ring_copy(stream, c, d, i).start()

    def finish(stream, ticks, c):
        for i in range(len(ticks) - 2, len(ticks)):
            for d in (1, -1):
                ring_copy(stream, c, d, i).wait_recv()

    def drain(stream, ticks, c):
        for i in range(len(ticks)):
            for d in (1, -1):
                ring_copy(stream, c, d, i).wait_send()

    def rows_of(n):
        return n // 4, pl.ds((n % 4) * 2, 2)

    def rotate(c, begin, count):
        def body(n, _):
            xn, zn = rows_of(n)
            high, low = split_terms(buf[c, xn, zn].reshape(256, GROUP))
            part = grad[pl.ds(n * 256, 256), :]
            dims = (((0,), (0,)), ((), ()))
            total = lax.dot_general(high, part, dims, preferred_element_type=jnp.float32)
            total += lax.dot_general(low, part, dims, preferred_element_type=jnp.float32)
            total = total.reshape(2, 2, QUARTER, COLS)

            @pl.when(n == 0)
            def _():
                partial[c] = total

            @pl.when(n > 0)
            def _():
                partial[c] += total
            return 0
        lax.fori_loop(begin, begin + count, body, 0)

    def rotate_back(c, last):
        a_high, a_low = split_terms(adjusted[c].reshape(GROUP, COLS))

        def body(n, _):
            xn, zn = rows_of(n)
            high, low = split_terms(buf[c, xn, zn].reshape(256, GROUP))
            here = pl.ds(n * 256, 256)
            total = jnp.dot(high, a_low, preferred_element_type=jnp.float32)
            total += jnp.dot(low, a_high, preferred_element_type=jnp.float32)
            total += jnp.dot(high, a_high, preferred_element_type=jnp.float32)
            update[here, :] += total

            @pl.when(last)
            def _():
                pltpu.make_async_copy(update.at[here], update_hbm.at[here], out_sem.at[n]).start()
            return 0
        lax.fori_loop(0, ROWS // 256, body, 0)

    def rs1_copy(c):
        return remote(partial.at[c, :, 1 - core], rs1.at[c], c, SEM_RS1, core_peer)

    def rs2_copy(c):
        return remote(xsend.at[c], rs2.at[c], c, SEM_RS2, chip_peer)

    def ax_copy(c):
        ref = adjusted.at[c, xlo, core]
        return remote(ref, ref, c, SEM_AX, chip_peer)

    def ac_copy(c):
        ref = adjusted.at[c, xlo, core]
        return remote(ref, ref, c, SEM_AC, core_peer)

    def af_copy(c):
        ref = adjusted.at[c, 1 - xlo, core]
        return remote(ref, ref, c, SEM_AF, core_peer)

    def moments(c):
        rotated = partial[c, xlo, core] + rs1[c, xlo] + rs2[c]
        one = beta_one * first_in[c] + (1.0 - beta_one) * rotated
        two = beta_two * second_in[c] + (1.0 - beta_two) * rotated * rotated
        first_out[c] = one
        second_out[c] = two
        adjusted[c, xlo, core] = one / correct_one / (jnp.sqrt(two / correct_two) + epsilon)

    def macro(m, _):
        do_p1 = m < GROUPS
        do_p2 = (m >= 1) & (m < GROUPS + 1)
        do_p2_left = (m >= 2) & (m < GROUPS + 2)
        do_mid = (m >= 2) & (m < GROUPS + 2)
        do_back = m >= 3
        s1, s2, s3, s4 = m, m - 1, m - 2, m - 3

        @pl.when(do_p1)
        def _():
            x_copy(s1).wait_recv()

        for t in range(TICKS):
            if t < TICKS - 1:
                @pl.when(do_p2)
                def _(t=t):
                    run_tick("b2", Z_TICKS, s2, t)
                    run_tick("a2", Y_BIG_TICKS, s2, t)

                @pl.when(do_p1)
                def _(t=t):
                    run_tick("a1", Z_TICKS, s1, t)
                    run_tick("b1", Y_SMALL_TICKS, s1, t)

            if t == 0:
                @pl.when(m == 2)
                def _():
                    grad_copy.wait()

                @pl.when(m == 3)
                def _():
                    prior_copy.wait()

                @pl.when(do_back)
                def _():
                    ac_copy(s4).wait_recv()
                    af_copy(s4).wait_recv()
                    rotate_back(s4, m == GROUPS + 2)
            if t == 1:
                @pl.when(do_p2_left)
                def _():
                    finish("a2", Y_BIG_TICKS, s3)
                    finish("b2", Z_TICKS, s3)
                    rotate(s3, 0, 4)
            if t == 2:
                @pl.when(do_mid)
                def _():
                    rotate(s3, 4, 4)
                    rs1_copy(s3).start()
            if t == 3:
                @pl.when(do_mid)
                def _():
                    rs1_copy(s3).wait_recv()
                    xsend[s3] = partial[s3, 1 - xlo, core] + rs1[s3, 1 - xlo]
                    rs2_copy(s3).start()
            if t == 5:
                @pl.when(do_mid)
                def _():
                    rs2_copy(s3).wait_recv()
                    moments(s3)
                    ax_copy(s3).start()
                    ac_copy(s3).start()
            if t == 7:
                @pl.when(do_p1)
                def _():
                    finish("a1", Z_TICKS, s1)
                    finish("b1", Y_SMALL_TICKS, s1)

                @pl.when(do_mid)
                def _():
                    ax_copy(s3).wait_recv()
                    af_copy(s3).start()
        return 0

    lax.fori_loop(0, GROUPS + 3, macro, 0)

    def last(c, _):
        x_copy(c).wait_send()
        drain("a1", Z_TICKS, c)
        drain("b1", Y_SMALL_TICKS, c)
        drain("a2", Y_BIG_TICKS, c)
        drain("b2", Z_TICKS, c)
        for copy in (rs1_copy, rs2_copy, ax_copy, ac_copy, af_copy):
            copy(c).wait_send()
        return 0

    lax.fori_loop(0, GROUPS, last, 0)

    def written(n, _):
        here = pl.ds(n * 256, 256)
        pltpu.make_async_copy(update.at[here], update_hbm.at[here], out_sem.at[n]).wait()
        return 0

    lax.fori_loop(0, ROWS // 256, written, 0)


def step(gradient, eigenbasis, first_moment, second_moment, prior_update, group_ids):
    pieces = lax.all_to_all(
        eigenbasis.reshape(NX * NZ * NY, PIECE, 128), "cols", 0, 0, tiled=True)
    vmem = pl.BlockSpec(memory_space=pltpu.VMEM)
    hbm = pl.BlockSpec(memory_space=pl.ANY)
    block = (GROUPS, QUARTER, COLS)
    return pl.pallas_call(
        kernel,
        out_shape=(
            jax.ShapeDtypeStruct(block, jnp.float32),
            jax.ShapeDtypeStruct(block, jnp.float32),
            jax.ShapeDtypeStruct((ROWS, COLS), jnp.float32),
        ),
        in_specs=[pl.BlockSpec(memory_space=pltpu.SMEM), vmem, vmem, vmem, hbm, hbm],
        out_specs=(vmem, vmem, hbm),
        scratch_shapes=[
            pltpu.VMEM((GROUPS, NX, NZ, NY, PIECE, GROUP), jnp.float32),
            pltpu.VMEM((ROWS, COLS), jnp.bfloat16),
            pltpu.VMEM((ROWS, COLS), jnp.float32),
            pltpu.VMEM((GROUPS, 2, 2, QUARTER, COLS), jnp.float32),
            pltpu.VMEM((GROUPS, 2, QUARTER, COLS), jnp.float32),
            pltpu.VMEM(block, jnp.float32),
            pltpu.VMEM(block, jnp.float32),
            pltpu.VMEM((GROUPS, 2, 2, QUARTER, COLS), jnp.float32),
            pltpu.SemaphoreType.DMA((GROUPS, SEMS)),
            pltpu.SemaphoreType.DMA((GROUPS, SEMS)),
            pltpu.SemaphoreType.DMA((2,)),
            pltpu.SemaphoreType.DMA((ROWS // 256,)),
        ],
        compiler_params=pltpu.CompilerParams(
            collective_id=0, has_side_effects=True, vmem_limit_bytes=50 * 1024 * 1024),
        cost_estimate=pl.CostEstimate(flops=9_400_000_000, bytes_accessed=14_000_000, transcendentals=0),
    )(group_ids, pieces, first_moment, second_moment, gradient, prior_update)


def solution(mesh):
    split = P("rows", "cols")
    moment = P(None, "rows", "cols")
    return jax.shard_map(
        step, mesh=mesh,
        in_specs=(split, split, moment, moment, split, P(None)),
        out_specs=(moment, moment, split),
        check_vma=False,
    )
```

```python
import functools

import jax
import jax.numpy as jnp
from jax import lax
from jax.experimental import pallas as pl
from jax.experimental.pallas import tpu as pltpu
from jax.sharding import PartitionSpec as P

MESH = pl.DeviceIdType.MESH

GROUPS = 4
NX, NZ, NY = 2, 8, 4
SPREAD = NX * NZ * NY
PIECE = 32
GROUP = 256
QUARTER = 64
COLS = 448
ROWS = 2048

beta_one = 0.9
beta_two = 0.95
correct_one = 1.0 - 0.9**10
correct_two = 1.0 - 0.95**10
epsilon = 1e-08

FIRST, SECOND = pl.ds(0, 16), pl.ds(16, 16)

SEM_X = 0
SEM_A1 = 1
SEM_B1 = SEM_A1 + 16
SEM_A2 = SEM_B1 + 8
SEM_B2 = SEM_A2 + 4
SEM_RS1 = SEM_B2 + 8
SEM_RS2 = SEM_RS1 + 1
SEM_AX = SEM_RS2 + 1
SEM_AC = SEM_AX + 1
SEM_AF = SEM_AC + 1
SEMS = SEM_AF + 1


def split_terms(value):
    high = value.astype(jnp.bfloat16)
    low = (value - high.astype(jnp.float32)).astype(jnp.bfloat16)
    return high, low


def kernel(ids, basis_hbm, first_in, second_in, grad_hbm, prior_hbm,
           first_out, second_out, update_hbm,
           pieces, buf, grad, update, rotated, partial, rs1, xsend, rs2, adjusted,
           send_sem, recv_sem, local_sem, out_sem, deal_send, deal_recv):
    cols = lax.axis_index("cols")
    rows = lax.axis_index("rows")
    xh = cols // (NZ * NY)
    z = (cols // NY) % NZ
    y = cols % NY
    xlo = rows // 2
    core = rows % 2
    sign = 1 - 2 * core

    def at(xh_, z_, y_):
        return (xh_ * NZ + z_) * NY + y_

    x_peer = (at(1 - xh, z, y), rows)
    z_peer = {d: (at(xh, (z + d * sign + NZ) % NZ, y), rows) for d in (1, -1)}
    y_peer = {d: (at(xh, z, (y + d * sign + NY) % NY), rows) for d in (1, -1)}
    core_peer = (cols, xlo * 2 + 1 - core)
    chip_peer = (cols, (1 - xlo) * 2 + core)

    grad_copy = pltpu.make_async_copy(grad_hbm, grad, local_sem.at[0])
    prior_copy = pltpu.make_async_copy(prior_hbm, update, local_sem.at[1])

    barrier = pltpu.get_barrier_semaphore()
    for peer in (core_peer, chip_peer):
        pl.semaphore_signal(barrier, inc=1, device_id=peer, device_id_type=MESH)

    def greet(n, _):
        pl.semaphore_signal(barrier, inc=1, device_id=((cols + n) % SPREAD, rows), device_id_type=MESH)
        return 0

    lax.fori_loop(1, SPREAD, greet, 0)
    pl.semaphore_wait(barrier, SPREAD + 1)

    def deal(n, _):
        to = (cols + n) % SPREAD
        pltpu.make_async_remote_copy(
            src_ref=basis_hbm.at[to], dst_ref=pieces.at[cols], send_sem=deal_send, recv_sem=deal_recv,
            device_id=(to, rows), device_id_type=MESH).start()
        return 0

    lax.fori_loop(1, SPREAD, deal, 0)
    own_piece = pltpu.make_async_copy(basis_hbm.at[cols], pieces.at[cols], local_sem.at[2])
    own_piece.start()
    grad_copy.start()
    prior_copy.start()
    own_piece.wait()
    others = pl.ds(0, SPREAD - 1)
    dealt = pltpu.make_async_remote_copy(
        src_ref=basis_hbm.at[others], dst_ref=pieces.at[others], send_sem=deal_send, recv_sem=deal_recv,
        device_id=((cols + 1) % SPREAD, rows), device_id_type=MESH)
    dealt.wait_recv()

    for c in range(GROUPS):
        for half in range(2):
            buf[c, xh, z, y, :, half * 128:(half + 1) * 128] = pieces[ids[c] * 2 + half]

    def remote(src, dst, c, number, peer):
        return pltpu.make_async_remote_copy(
            src_ref=src, dst_ref=dst, send_sem=send_sem.at[c, number], recv_sem=recv_sem.at[c, number],
            device_id=peer, device_id_type=MESH)

    def x_copy():
        ref = buf.at[:, xh, z, y]
        return remote(ref, ref, 0, SEM_X, x_peer)

    own, other = xh, 1 - xh

    def zk(d, k):
        return (z - d * sign * k + NZ) % NZ

    def yk(d, k):
        return (y - d * sign * k + 2 * NY) % NY

    def spread_z(half, d, k):
        which, lane = (0, own) if half == 0 else (1, other)
        ref = buf.at[:, lane, zk(d, k), y, FIRST]
        return remote(ref, ref, 0, SEM_A1 + which * 8 + (0 if d == 1 else 4) + k, z_peer[d])

    def spread_y(half, d, k):
        which, lane = (0, own) if half == 0 else (1, other)
        ref = buf.at[:, lane, z, yk(d, k), SECOND]
        return remote(ref, ref, 0, SEM_B1 + which * 4 + (0 if d == 1 else 2) + k, y_peer[d])

    z_steps = [(half, d, k) for k in range(4) for half in range(2) for d in (1, -1)
               if k < 3 or (half == 0) == (d == 1)]
    y_steps = [(half, d, k) for k in range(2) for half in range(2) for d in (1, -1)
               if k < 1 or (half == 0) == (d == 1)]

    def lanes(d, whole):
        return slice(None) if whole else (0 if d == 1 else 1)

    def gather_z(c, d, k):
        ref = buf.at[c, lanes(d, k < 3), zk(d, k), :, SECOND]
        return remote(ref, ref, c, SEM_B2 + (0 if d == 1 else 4) + k, z_peer[d])

    def gather_y(c, d, k):
        ref = buf.at[c, lanes(d, k < 1), :, yk(d, k), FIRST]
        return remote(ref, ref, c, SEM_A2 + (0 if d == 1 else 2) + k, y_peer[d])

    def both(make, c, k, action):
        for d in (1, -1):
            getattr(make(c, d, k), action)()

    def rows_of(n):
        return n // 4, pl.ds((n % 4) * 2, 2)

    def rotate(c, half):
        high, low = split_terms(buf[c, half].reshape(ROWS // 2, GROUP))
        part = grad[:, half * (ROWS // 2):(half + 1) * (ROWS // 2)]
        total = jnp.dot(part, high, preferred_element_type=jnp.float32)
        total += jnp.dot(part, low, preferred_element_type=jnp.float32)
        if half == 0:
            rotated[...] = total
        else:
            partial[c] = (rotated[...] + total).T.reshape(2, 2, QUARTER, COLS)

    def rotate_back(c, last):
        a_high, a_low = split_terms(adjusted[c].reshape(GROUP, COLS).T)
        dims = (((1,), (1,)), ((), ()))

        def body(n, _):
            xn, zn = rows_of(n)
            high, low = split_terms(buf[c, xn, zn].reshape(256, GROUP))
            here = pl.ds(pl.multiple_of(n * 256, 256), 256)
            total = lax.dot_general(a_low, high, dims, preferred_element_type=jnp.float32)
            total += lax.dot_general(a_high, low, dims, preferred_element_type=jnp.float32)
            total += lax.dot_general(a_high, high, dims, preferred_element_type=jnp.float32)
            update[:, here] += total

            if last:
                pltpu.make_async_copy(update.at[:, here], update_hbm.at[:, here], out_sem.at[n]).start()
            return 0
        lax.fori_loop(0, ROWS // 256, body, 0)

    def rs1_copy(c):
        return remote(partial.at[c, :, 1 - core], rs1.at[c], c, SEM_RS1, core_peer)

    def rs2_copy(c):
        return remote(xsend.at[c], rs2.at[c], c, SEM_RS2, chip_peer)

    def ax_copy(c):
        ref = adjusted.at[c, xlo, core]
        return remote(ref, ref, c, SEM_AX, chip_peer)

    def ac_copy(c):
        ref = adjusted.at[c, xlo, core]
        return remote(ref, ref, c, SEM_AC, core_peer)

    def af_copy(c):
        ref = adjusted.at[c, 1 - xlo, core]
        return remote(ref, ref, c, SEM_AF, core_peer)

    def moments(c):
        mine = partial[c, xlo, core] + rs1[c, xlo] + rs2[c]
        one = beta_one * first_in[c] + (1.0 - beta_one) * mine
        two = beta_two * second_in[c] + (1.0 - beta_two) * mine * mine
        first_out[c] = one
        second_out[c] = two
        adjusted[c, xlo, core] = one / correct_one / (jnp.sqrt(two / correct_two) + epsilon)

    def z_step(c, k):
        if k > 0:
            both(gather_z, c, k - 1, "wait_recv")
        both(gather_z, c, k, "start")

    def y_step(c, k):
        if k > 0:
            both(gather_y, c, k - 1, "wait_recv")
        both(gather_y, c, k, "start")

    def arrive(c):
        both(gather_z, c, 3, "wait_recv")
        both(gather_y, c, 1, "wait_recv")
        rotate(c, 0)
        rotate(c, 1)
        rs1_copy(c).start()

    def cross(c):
        rs1_copy(c).wait_recv()
        xsend[c] = partial[c, 1 - xlo, core] + rs1[c, 1 - xlo]
        rs2_copy(c).start()

    def adjust(c):
        rs2_copy(c).wait_recv()
        moments(c)
        ax_copy(c).start()
        ac_copy(c).start()

    def forward(c):
        ax_copy(c).wait_recv()
        af_copy(c).start()

    def back(c):
        ac_copy(c).wait_recv()
        af_copy(c).wait_recv()
        rotate_back(c, c == GROUPS - 1)

    def spread_step(make, steps, k):
        for half in range(2):
            for d in (1, -1):
                if k > 0 and (half, d, k - 1) in steps:
                    make(half, d, k - 1).wait_recv()
                if (half, d, k) in steps:
                    make(half, d, k).start()

    x_copy().start()
    for half in range(2):
        if half == 1:
            x_copy().wait_recv()
        for d in (1, -1):
            spread_z(half, d, 0).start()
            spread_y(half, d, 0).start()
    spread_step(spread_y, y_steps, 1)
    spread_step(spread_z, z_steps, 1)
    spread_step(spread_y, y_steps, 2)
    z_step(0, 0)
    spread_step(spread_z, z_steps, 2)
    z_step(1, 0)
    spread_step(spread_z, z_steps, 3)
    z_step(0, 1)
    spread_step(spread_z, z_steps, 4)

    y_step(0, 0)
    z_step(1, 1)
    z_step(0, 2)
    y_step(1, 0)
    z_step(2, 0)
    y_step(0, 1)
    z_step(0, 3)
    z_step(1, 2)
    y_step(2, 0)
    z_step(2, 1)
    y_step(1, 1)
    z_step(1, 3)
    z_step(3, 0)
    grad_copy.wait()
    prior_copy.wait()
    arrive(0)
    z_step(2, 2)
    y_step(3, 0)
    cross(0)
    z_step(3, 1)
    y_step(2, 1)
    arrive(1)
    adjust(0)
    z_step(2, 3)
    cross(1)
    z_step(3, 2)
    y_step(3, 1)
    forward(0)
    arrive(2)
    adjust(1)
    back(0)
    z_step(3, 3)
    cross(2)
    forward(1)
    adjust(2)
    arrive(3)
    back(1)
    cross(3)
    forward(2)
    back(2)
    adjust(3)
    forward(3)
    back(3)

    dealt.wait_send()
    x_copy().wait_send()
    for step_ in z_steps:
        spread_z(*step_).wait_send()
    for step_ in y_steps:
        spread_y(*step_).wait_send()

    def last(c, _):
        for k in range(4):
            both(gather_z, c, k, "wait_send")
        for k in range(2):
            both(gather_y, c, k, "wait_send")
        for copy in (rs1_copy, rs2_copy, ax_copy, ac_copy, af_copy):
            copy(c).wait_send()
        return 0

    lax.fori_loop(0, GROUPS, last, 0)

    def written(n, _):
        here = pl.ds(pl.multiple_of(n * 256, 256), 256)
        pltpu.make_async_copy(update.at[:, here], update_hbm.at[:, here], out_sem.at[n]).wait()
        return 0

    lax.fori_loop(0, ROWS // 256, written, 0)


def step(gradient, eigenbasis, first_moment, second_moment, prior_update, group_ids):
    pieces = eigenbasis.reshape(SPREAD, PIECE, 128)
    vmem = pl.BlockSpec(memory_space=pltpu.VMEM)
    hbm = pl.BlockSpec(memory_space=pl.ANY)
    block = (GROUPS, QUARTER, COLS)
    first_out, second_out, update = pl.pallas_call(
        kernel,
        out_shape=(
            jax.ShapeDtypeStruct(block, jnp.float32),
            jax.ShapeDtypeStruct(block, jnp.float32),
            jax.ShapeDtypeStruct((COLS, ROWS), jnp.float32),
        ),
        in_specs=[pl.BlockSpec(memory_space=pltpu.SMEM), hbm, vmem, vmem, hbm, hbm],
        out_specs=(vmem, vmem, hbm),
        scratch_shapes=[
            pltpu.VMEM((SPREAD, PIECE, 128), jnp.float32),
            pltpu.VMEM((GROUPS, NX, NZ, NY, PIECE, GROUP), jnp.float32),
            pltpu.VMEM((COLS, ROWS), jnp.bfloat16),
            pltpu.VMEM((COLS, ROWS), jnp.float32),
            pltpu.VMEM((COLS, GROUP), jnp.float32),
            pltpu.VMEM((GROUPS, 2, 2, QUARTER, COLS), jnp.float32),
            pltpu.VMEM((GROUPS, 2, QUARTER, COLS), jnp.float32),
            pltpu.VMEM(block, jnp.float32),
            pltpu.VMEM(block, jnp.float32),
            pltpu.VMEM((GROUPS, 2, 2, QUARTER, COLS), jnp.float32),
            pltpu.SemaphoreType.DMA((GROUPS, SEMS)),
            pltpu.SemaphoreType.DMA((GROUPS, SEMS)),
            pltpu.SemaphoreType.DMA((3,)),
            pltpu.SemaphoreType.DMA((ROWS // 256,)),
            pltpu.SemaphoreType.DMA,
            pltpu.SemaphoreType.DMA,
        ],
        compiler_params=pltpu.CompilerParams(
            collective_id=0, has_side_effects=True, vmem_limit_bytes=50 * 1024 * 1024),
        cost_estimate=pl.CostEstimate(flops=9_400_000_000, bytes_accessed=14_000_000, transcendentals=0),
    )(group_ids, pieces, first_moment, second_moment, gradient.T, prior_update.T)
    return first_out, second_out, update.T


def solution(mesh):
    split = P("rows", "cols")
    moment = P(None, "rows", "cols")
    return jax.shard_map(
        step, mesh=mesh,
        in_specs=(split, split, moment, moment, split, P(None)),
        out_specs=(moment, moment, split),
        check_vma=False,
    )
```

```python
import functools

import jax
import jax.numpy as jnp
from jax import lax
from jax.experimental import pallas as pl
from jax.experimental.pallas import tpu as pltpu
from jax.sharding import PartitionSpec as P

MESH = pl.DeviceIdType.MESH

GROUPS = 4
NX, NZ, NY = 2, 8, 4
SPREAD = NX * NZ * NY
PIECE = 32
GROUP = 256
QUARTER = 64
COLS = 448
ROWS = 2048

beta_one = 0.9
beta_two = 0.95
correct_one = 1.0 - 0.9**10
correct_two = 1.0 - 0.95**10
epsilon = 1e-08

FIRST, SECOND = pl.ds(0, 16), pl.ds(16, 16)

SEM_A2 = 0
SEM_B2 = SEM_A2 + 4
SEM_RS1 = SEM_B2 + 8
SEM_RS2 = SEM_RS1 + 1
SEM_AX = SEM_RS2 + 2
SEM_AC = SEM_AX + 2
SEM_AF = SEM_AC + 2
SEMS = SEM_AF + 2


def split_terms(value):
    high = value.astype(jnp.bfloat16)
    low = (value - high.astype(jnp.float32)).astype(jnp.bfloat16)
    return high, low


def back_product(a_high, a_low, high, low):
    dims = (((1,), (1,)), ((), ()))
    total = lax.dot_general(a_low, high, dims, preferred_element_type=jnp.float32)
    total += lax.dot_general(a_high, low, dims, preferred_element_type=jnp.float32)
    return total + lax.dot_general(a_high, high, dims, preferred_element_type=jnp.float32)


def kernel(ids, basis_hbm, first_hbm, second_hbm, grad_hbm, prior_hbm,
           first_out, second_out, update, terms_out, adjusted_out,
           pieces, buf, grad, rotated, partial, rs1, xsend, rs2, adjusted,
           send_sem, recv_sem, local_sem, deal_send, deal_recv,
           spread_send, spread_recv, first_in, second_in, met):
    cols = lax.axis_index("cols")
    rows = lax.axis_index("rows")
    xh = cols // (NZ * NY)
    z = (cols // NY) % NZ
    y = cols % NY
    xlo = rows // 2
    core = rows % 2
    sign = 1 - 2 * core

    def at(xh_, z_, y_):
        return (xh_ * NZ + z_) * NY + y_

    x_peer = (at(1 - xh, z, y), rows)
    z_peer = {d: (at(xh, (z + d * sign + NZ) % NZ, y), rows) for d in (1, -1)}
    y_peer = {d: (at(xh, z, (y + d * sign + NY) % NY), rows) for d in (1, -1)}
    core_peer = (cols, xlo * 2 + 1 - core)
    chip_peer = (cols, (1 - xlo) * 2 + core)

    grad_copy = pltpu.make_async_copy(grad_hbm, grad, local_sem.at[0])
    prior_copy = pltpu.make_async_copy(prior_hbm, update, local_sem.at[1])
    first_copy = pltpu.make_async_copy(first_hbm, first_in, local_sem.at[3])
    second_copy = pltpu.make_async_copy(second_hbm, second_in, local_sem.at[4])

    def place(j, k, l):
        return (((xh + j) % NX) * NZ + (z + k) % NZ) * NY + (y + l) % NY

    def deal(j, k, l):
        to = place(j, k, l)
        pltpu.make_async_remote_copy(
            src_ref=basis_hbm.at[to], dst_ref=pieces.at[cols], send_sem=deal_send, recv_sem=deal_recv,
            device_id=(to, rows), device_id_type=MESH).start()

    line = [(0, k, 0) for k in range(1, NZ)] + [(0, 0, l) for l in range(1, NY)] + [(1, 0, 0)]
    barrier = pltpu.get_barrier_semaphore()
    for offsets in line:
        pl.semaphore_signal(barrier, inc=1, device_id=(place(*offsets), rows), device_id_type=MESH)
    for peer in (core_peer, chip_peer):
        pl.semaphore_signal(barrier, inc=1, device_id=peer, device_id_type=MESH)
    pl.semaphore_wait(barrier, len(line) + 2)
    for l in range(1, NY):
        pl.semaphore_signal(met.at[0], inc=1, device_id=(place(0, 0, l), rows), device_id_type=MESH)
    for offsets in line:
        deal(*offsets)
    pl.semaphore_wait(met.at[0], NY - 1)
    pl.semaphore_signal(met.at[1], inc=1, device_id=x_peer, device_id_type=MESH)
    for k in range(1, NZ):
        for l in range(1, NY):
            deal(0, k, l)
    pl.semaphore_wait(met.at[1], 1)
    for k in range(NZ):
        for l in range(NY):
            if (k, l) != (0, 0):
                deal(1, k, l)
    own_piece = pltpu.make_async_copy(basis_hbm.at[cols], pieces.at[cols], local_sem.at[2])
    own_piece.start()
    grad_copy.start()
    prior_copy.start()
    first_copy.start()
    second_copy.start()
    own_piece.wait()
    others = pl.ds(0, SPREAD - 1)
    dealt = pltpu.make_async_remote_copy(
        src_ref=basis_hbm.at[others], dst_ref=pieces.at[others], send_sem=deal_send, recv_sem=deal_recv,
        device_id=((cols + 1) % SPREAD, rows), device_id_type=MESH)
    dealt.wait_recv()

    for c in range(GROUPS):
        for half in range(2):
            buf[c, xh, z, y, :, half * 128:(half + 1) * 128] = pieces[ids[c] * 2 + half]

    def remote(src, dst, c, number, peer):
        return pltpu.make_async_remote_copy(
            src_ref=src, dst_ref=dst, send_sem=send_sem.at[c, number], recv_sem=recv_sem.at[c, number],
            device_id=peer, device_id_type=MESH)

    def zk(d, k):
        return (z - d * sign * k + NZ) % NZ

    def yk(d, k):
        return (y - d * sign * k + 2 * NY) % NY

    def spread(src, p, number, peer):
        return pltpu.make_async_remote_copy(
            src_ref=src, dst_ref=src, send_sem=spread_send.at[p, number], recv_sem=spread_recv.at[p, number],
            device_id=peer, device_id_type=MESH)

    def z_block(p, j):
        return buf.at[pl.ds(2 * p, 2), xh, zk(1, -j), y, FIRST]

    def z_near(p, j):
        return spread(z_block(p, 0), p, 2 + j if j < 0 else 1 + j, (at(xh, zk(1, -j), y), rows))

    def z_third(p, d):
        return spread(z_block(p, -2 * d), p, 4 if d == 1 else 5, (at(xh, zk(1, -d), y), rows))

    def z_fourth(p, d):
        src = buf.at[2 * p + (0 if d == 1 else 1), xh, zk(1, 2 * d), y, FIRST]
        return spread(src, p, 6 if d == 1 else 7, (at(xh, zk(1, -2 * d), y), rows))

    def z_across(p, j):
        return spread(z_block(p, j), p, 8 + j % NZ, x_peer)

    def y_near(p, j):
        return spread(buf.at[pl.ds(2 * p, 2), xh, z, y, SECOND], p, 15 + j, (at(xh, z, (y + j) % NY), rows))

    def y_across(p):
        return spread(buf.at[pl.ds(2 * p, 2), xh, z, :, SECOND], p, 19, x_peer)

    def spread_begin(p):
        for j in (1, 2, 3):
            y_near(p, j).start()
        for j in (1, -1, 2, -2):
            z_near(p, j).start()
        z_across(p, 0).start()

    def spread_y(p):
        for j in (1, 2, 3):
            y_near(p, j).wait_recv()
        y_across(p).start()

    def spread_z(p):
        for d in (1, -1):
            z_near(p, 2 * d).wait_recv()
            z_third(p, d).start()
            z_fourth(p, d).start()
            z_across(p, -2 * d).start()
        for d in (1, -1):
            z_near(p, d).wait_recv()
            z_across(p, -d).start()

    def spread_far(p):
        for d in (1, -1):
            z_third(p, d).wait_recv()
            z_across(p, -3 * d).start()
        for d in (1, -1):
            z_fourth(p, d).wait_recv()
        z_across(p, 4).start()

    def spread_z_ready(p):
        for j in (0, -2, 2, -1, 1, -3, 3, 4):
            z_across(p, j).wait_recv()

    def spread_drain(p):
        for d in (1, -1):
            for copy in (z_near(p, d), z_near(p, 2 * d), z_third(p, d), z_fourth(p, d)):
                copy.wait_send()
        for j in range(NZ):
            z_across(p, j - 3).wait_send()
        for j in (1, 2, 3):
            y_near(p, j).wait_send()
        y_across(p).wait_send()

    def lanes(d, whole):
        return slice(None) if whole else (0 if d == 1 else 1)

    def gather_z(c, d, k):
        ref = buf.at[c, lanes(d, k < 3), zk(d, k), :, SECOND]
        return remote(ref, ref, c, SEM_B2 + (0 if d == 1 else 4) + k, z_peer[d])

    def gather_y(c, d, k):
        ref = buf.at[c, lanes(d, k < 1), :, yk(d, k), FIRST]
        return remote(ref, ref, c, SEM_A2 + (0 if d == 1 else 2) + k, y_peer[d])

    def both(make, c, k, action):
        for d in (1, -1):
            getattr(make(c, d, k), action)()

    def rows_of(n):
        return n // 4, pl.ds((n % 4) * 2, 2)

    def rotate(c, half):
        high, low = split_terms(buf[c, half].reshape(ROWS // 2, GROUP))
        if c == GROUPS - 1:
            here = slice(half * (ROWS // 2), (half + 1) * (ROWS // 2))
            terms_out[0, here, :] = high
            terms_out[1, here, :] = low
        part = grad[:, half * (ROWS // 2):(half + 1) * (ROWS // 2)]
        total = jnp.dot(part, high, preferred_element_type=jnp.float32)
        total += jnp.dot(part, low, preferred_element_type=jnp.float32)
        if half == 0:
            rotated[...] = total
        else:
            partial[c] = (rotated[...] + total).T.reshape(2, 2, QUARTER, COLS)

    def rotate_back(c):
        a_high, a_low = split_terms(adjusted[c].reshape(GROUP, COLS).T)

        def body(n, _):
            xn, zn = rows_of(n)
            high, low = split_terms(buf[c, xn, zn].reshape(256, GROUP))
            here = pl.ds(pl.multiple_of(n * 256, 256), 256)
            update[:, here] += back_product(a_high, a_low, high, low)
            return 0
        lax.fori_loop(0, ROWS // 256, body, 0)

    def rs1_copy(c):
        return remote(partial.at[c, :, 1 - core], rs1.at[c], c, SEM_RS1, core_peer)

    def half_rows(i):
        return pl.ds(i * (QUARTER // 2), QUARTER // 2)

    def rs2_copy(c, i):
        return remote(xsend.at[c, half_rows(i)], rs2.at[c, half_rows(i)], c, SEM_RS2 + i, chip_peer)

    def ax_copy(c, i):
        ref = adjusted.at[c, xlo, core, half_rows(i)]
        return remote(ref, ref, c, SEM_AX + i, chip_peer)

    def ac_copy(c, i):
        ref = adjusted.at[c, xlo, core, half_rows(i)]
        return remote(ref, ref, c, SEM_AC + i, core_peer)

    def af_copy(c, i):
        ref = adjusted.at[c, 1 - xlo, core, half_rows(i)]
        return remote(ref, ref, c, SEM_AF + i, core_peer)

    def moments(c, i):
        part = half_rows(i)
        mine = partial[c, xlo, core, part] + rs1[c, xlo, part] + rs2[c, part]
        one = beta_one * first_in[c, part] + (1.0 - beta_one) * mine
        two = beta_two * second_in[c, part] + (1.0 - beta_two) * mine * mine
        first_out[c, part] = one
        second_out[c, part] = two
        adjusted[c, xlo, core, part] = one / correct_one / (jnp.sqrt(two / correct_two) + epsilon)

    def z_step(c, k):
        if k > 0:
            both(gather_z, c, k - 1, "wait_recv")
        both(gather_z, c, k, "start")

    def y_step(c, k):
        if k > 0:
            both(gather_y, c, k - 1, "wait_recv")
        both(gather_y, c, k, "start")

    def arrive(c):
        both(gather_z, c, 3, "wait_recv")
        both(gather_y, c, 1, "wait_recv")
        rotate(c, 0)
        rotate(c, 1)
        rs1_copy(c).start()

    def cross(c):
        rs1_copy(c).wait_recv()
        for i in range(2):
            part = half_rows(i)
            xsend[c, part] = partial[c, 1 - xlo, core, part] + rs1[c, 1 - xlo, part]
            rs2_copy(c, i).start()

    def adjust(c):
        for i in range(2):
            rs2_copy(c, i).wait_recv()
            moments(c, i)
            ax_copy(c, i).start()
            ac_copy(c, i).start()

    def forward(c):
        for i in range(2):
            ax_copy(c, i).wait_recv()
            af_copy(c, i).start()

    def adjusted_ready(c):
        for i in range(2):
            ac_copy(c, i).wait_recv()
            af_copy(c, i).wait_recv()

    def back(c):
        adjusted_ready(c)
        rotate_back(c)

    spread_begin(0)
    spread_y(0)
    spread_begin(1)
    spread_z(0)
    y_across(0).wait_recv()
    z_step(0, 0)
    spread_far(0)
    spread_y(1)
    z_step(1, 0)
    spread_z(1)
    spread_z_ready(0)

    y_step(0, 0)
    z_step(0, 1)
    y_step(1, 0)
    spread_far(1)
    z_step(1, 1)
    y_across(1).wait_recv()
    z_step(0, 2)
    z_step(2, 0)
    y_step(0, 1)
    z_step(0, 3)
    z_step(1, 2)
    spread_z_ready(1)
    y_step(2, 0)
    z_step(2, 1)
    y_step(1, 1)
    z_step(1, 3)
    z_step(3, 0)
    grad_copy.wait()
    prior_copy.wait()
    first_copy.wait()
    second_copy.wait()
    arrive(0)
    z_step(2, 2)
    y_step(3, 0)
    cross(0)
    z_step(3, 1)
    y_step(2, 1)
    arrive(1)
    adjust(0)
    z_step(2, 3)
    cross(1)
    z_step(3, 2)
    y_step(3, 1)
    forward(0)
    arrive(2)
    adjust(1)
    back(0)
    z_step(3, 3)
    cross(2)
    forward(1)
    adjust(2)
    arrive(3)
    back(1)
    cross(3)
    forward(2)
    back(2)
    adjust(3)
    forward(3)
    adjusted_ready(3)
    adjusted_out[...] = adjusted[3]

    dealt.wait_send()
    for p in range(2):
        spread_drain(p)

    for c in range(GROUPS):
        for k in range(4):
            both(gather_z, c, k, "wait_send")
        for k in range(2):
            both(gather_y, c, k, "wait_send")
        rs1_copy(c).wait_send()
        for copy in (rs2_copy, ax_copy, ac_copy, af_copy):
            for i in range(2):
                copy(c, i).wait_send()


def finish_kernel(first_in, second_in, update, terms, adjusted, first_out, second_out, update_out, result, sem):
    copies = [pltpu.make_async_copy(first_in, first_out, sem.at[ROWS // 256]),
              pltpu.make_async_copy(second_in, second_out, sem.at[ROWS // 256 + 1])]
    for copy in copies:
        copy.start()
    a_high, a_low = split_terms(adjusted[...].reshape(GROUP, COLS).T)
    for n in range(ROWS // 256):
        here = slice(n * 256, (n + 1) * 256)
        result[:, here] = update[:, here] + back_product(a_high, a_low, terms[0, here, :], terms[1, here, :])
        copies.append(pltpu.make_async_copy(result.at[:, here], update_out.at[:, here], sem.at[n]))
        copies[-1].start()
    for copy in copies:
        copy.wait()


def step(gradient, eigenbasis, first_moment, second_moment, prior_update, group_ids):
    pieces = eigenbasis.reshape(SPREAD, PIECE, 128)
    vmem = pl.BlockSpec(memory_space=pltpu.VMEM)
    hbm = pl.BlockSpec(memory_space=pl.ANY)
    block = (GROUPS, QUARTER, COLS)
    passed = pl.pallas_call(
        kernel,
        out_shape=(
            jax.ShapeDtypeStruct(block, jnp.float32),
            jax.ShapeDtypeStruct(block, jnp.float32),
            jax.ShapeDtypeStruct((COLS, ROWS), jnp.float32),
            jax.ShapeDtypeStruct((2, ROWS, GROUP), jnp.bfloat16),
            jax.ShapeDtypeStruct((2, 2, QUARTER, COLS), jnp.float32),
        ),
        in_specs=[pl.BlockSpec(memory_space=pltpu.SMEM), hbm, hbm, hbm, hbm, hbm],
        out_specs=(vmem,) * 5,
        scratch_shapes=[
            pltpu.VMEM((SPREAD, PIECE, 128), jnp.float32),
            pltpu.VMEM((GROUPS, NX, NZ, NY, PIECE, GROUP), jnp.float32),
            pltpu.VMEM((COLS, ROWS), jnp.bfloat16),
            pltpu.VMEM((COLS, GROUP), jnp.float32),
            pltpu.VMEM((GROUPS, 2, 2, QUARTER, COLS), jnp.float32),
            pltpu.VMEM((GROUPS, 2, QUARTER, COLS), jnp.float32),
            pltpu.VMEM(block, jnp.float32),
            pltpu.VMEM(block, jnp.float32),
            pltpu.VMEM((GROUPS, 2, 2, QUARTER, COLS), jnp.float32),
            pltpu.SemaphoreType.DMA((GROUPS, SEMS)),
            pltpu.SemaphoreType.DMA((GROUPS, SEMS)),
            pltpu.SemaphoreType.DMA((5,)),
            pltpu.SemaphoreType.DMA,
            pltpu.SemaphoreType.DMA,
            pltpu.SemaphoreType.DMA((2, 20)),
            pltpu.SemaphoreType.DMA((2, 20)),
            pltpu.VMEM(block, jnp.float32),
            pltpu.VMEM(block, jnp.float32),
            pltpu.SemaphoreType.REGULAR((2,)),
        ],
        compiler_params=pltpu.CompilerParams(
            collective_id=0, has_side_effects=True, vmem_limit_bytes=42 * 1024 * 1024),
        cost_estimate=pl.CostEstimate(flops=9_400_000_000, bytes_accessed=14_000_000, transcendentals=0),
    )(group_ids, pieces, first_moment, second_moment, gradient.T, prior_update.T)
    first_out, second_out, update = pl.pallas_call(
        finish_kernel,
        out_shape=(
            jax.ShapeDtypeStruct(block, jnp.float32),
            jax.ShapeDtypeStruct(block, jnp.float32),
            jax.ShapeDtypeStruct((COLS, ROWS), jnp.float32),
        ),
        in_specs=[vmem] * 5,
        out_specs=(hbm,) * 3,
        scratch_shapes=[pltpu.VMEM((COLS, ROWS), jnp.float32), pltpu.SemaphoreType.DMA((ROWS // 256 + 2,))],
        compiler_params=pltpu.CompilerParams(vmem_limit_bytes=24 * 1024 * 1024),
        cost_estimate=pl.CostEstimate(flops=1_400_000_000, bytes_accessed=5_000_000, transcendentals=0),
    )(*passed)
    return first_out, second_out, update.T


def solution(mesh):
    split = P("rows", "cols")
    moment = P(None, "rows", "cols")
    return jax.shard_map(
        step, mesh=mesh,
        in_specs=(split, split, moment, moment, split, P(None)),
        out_specs=(moment, moment, split),
        check_vma=False,
    )
```

```python
import functools

import jax
import jax.numpy as jnp
from jax import lax
from jax.experimental import pallas as pl
from jax.experimental.pallas import tpu as pltpu
from jax.sharding import PartitionSpec as P

MESH = pl.DeviceIdType.MESH

GROUPS = 4
NX, NZ, NY = 2, 8, 4
SPREAD = NX * NZ * NY
PIECE = 32
GROUP = 256
QUARTER = 64
COLS = 448
ROWS = 2048

beta_one = 0.9
beta_two = 0.95
correct_one = 1.0 - 0.9**10
correct_two = 1.0 - 0.95**10
epsilon = 1e-08

FIRST, SECOND = pl.ds(0, 16), pl.ds(16, 16)

SEM_A2 = 0
SEM_B2 = SEM_A2 + 6
SEM_RS1 = SEM_B2 + 10
SEM_RS2 = SEM_RS1 + 1
SEM_AX = SEM_RS2 + 2
SEM_AC = SEM_AX + 2
SEM_AF = SEM_AC + 2
SEMS = SEM_AF + 2


def split_terms(value):
    high = value.astype(jnp.bfloat16)
    low = (value - high.astype(jnp.float32)).astype(jnp.bfloat16)
    return high, low


def back_product(a_high, a_low, high, low):
    dims = (((1,), (1,)), ((), ()))
    total = lax.dot_general(a_low, high, dims, preferred_element_type=jnp.float32)
    total += lax.dot_general(a_high, low, dims, preferred_element_type=jnp.float32)
    return total + lax.dot_general(a_high, high, dims, preferred_element_type=jnp.float32)


def kernel(ids, basis_hbm, first_hbm, second_hbm, grad_hbm, prior_hbm,
           first_out, second_out, adjusted_out, update_out, terms_out,
           pieces, buf, grad, rotated, partial, rs1, xsend, rs2, adjusted,
           send_sem, recv_sem, local_sem, deal_send, deal_recv,
           spread_send, spread_recv, first_in, second_in, met, update, terms):
    cols = lax.axis_index("cols")
    rows = lax.axis_index("rows")
    xh = cols // (NZ * NY)
    z = (cols // NY) % NZ
    y = cols % NY
    xlo = rows // 2
    core = rows % 2
    sign = 1 - 2 * core

    def at(xh_, z_, y_):
        return (xh_ * NZ + z_) * NY + y_

    own, other = xh, 1 - xh
    x_peer = (at(1 - xh, z, y), rows)
    z_peer = {d: (at(xh, (z + d * sign + NZ) % NZ, y), rows) for d in (1, -1)}
    y_peer = {d: (at(xh, z, (y + d * sign + NY) % NY), rows) for d in (1, -1)}
    core_peer = (cols, xlo * 2 + 1 - core)
    chip_peer = (cols, (1 - xlo) * 2 + core)

    update_copy = pltpu.make_async_copy(update, update_out, local_sem.at[5])
    terms_copy = pltpu.make_async_copy(terms, terms_out, local_sem.at[6])
    grad_copy = pltpu.make_async_copy(grad_hbm, grad, local_sem.at[0])
    prior_copy = pltpu.make_async_copy(prior_hbm, update, local_sem.at[1])
    first_copy = pltpu.make_async_copy(first_hbm, first_in, local_sem.at[3])
    second_copy = pltpu.make_async_copy(second_hbm, second_in, local_sem.at[4])

    def place(j, k, l):
        return (((xh + j) % NX) * NZ + (z + k) % NZ) * NY + (y + l) % NY

    def deal(j, k, l):
        to = place(j, k, l)
        pltpu.make_async_remote_copy(
            src_ref=basis_hbm.at[to], dst_ref=pieces.at[cols], send_sem=deal_send, recv_sem=deal_recv,
            device_id=(to, rows), device_id_type=MESH).start()

    line = [(0, k, 0) for k in range(1, NZ)] + [(0, 0, l) for l in range(1, NY)] + [(1, 0, 0)]
    barrier = pltpu.get_barrier_semaphore()
    for offsets in line:
        pl.semaphore_signal(barrier, inc=1, device_id=(place(*offsets), rows), device_id_type=MESH)
    for peer in (core_peer, chip_peer):
        pl.semaphore_signal(barrier, inc=1, device_id=peer, device_id_type=MESH)
    pl.semaphore_wait(barrier, len(line) + 2)
    for l in range(1, NY):
        pl.semaphore_signal(met.at[0], inc=1, device_id=(place(0, 0, l), rows), device_id_type=MESH)
    for offsets in line:
        deal(*offsets)
    pl.semaphore_wait(met.at[0], NY - 1)
    pl.semaphore_signal(met.at[1], inc=1, device_id=x_peer, device_id_type=MESH)
    for k in range(1, NZ):
        for l in range(1, NY):
            deal(0, k, l)
    pl.semaphore_wait(met.at[1], 1)
    for k in range(NZ):
        for l in range(NY):
            if (k, l) != (0, 0):
                deal(1, k, l)
    own_piece = pltpu.make_async_copy(basis_hbm.at[cols], pieces.at[cols], local_sem.at[2])
    own_piece.start()
    grad_copy.start()
    prior_copy.start()
    first_copy.start()
    second_copy.start()
    own_piece.wait()
    others = pl.ds(0, SPREAD - 1)
    dealt = pltpu.make_async_remote_copy(
        src_ref=basis_hbm.at[others], dst_ref=pieces.at[others], send_sem=deal_send, recv_sem=deal_recv,
        device_id=((cols + 1) % SPREAD, rows), device_id_type=MESH)
    dealt.wait_recv()

    for c in range(GROUPS):
        for half in range(2):
            buf[c, xh, z, y, :, half * 128:(half + 1) * 128] = pieces[ids[c] * 2 + half]

    def remote(src, dst, c, number, peer):
        return pltpu.make_async_remote_copy(
            src_ref=src, dst_ref=dst, send_sem=send_sem.at[c, number], recv_sem=recv_sem.at[c, number],
            device_id=peer, device_id_type=MESH)

    def zk(d, k):
        return (z - d * sign * k + NZ) % NZ

    def yk(d, k):
        return (y - d * sign * k + 2 * NY) % NY

    def spread(src, p, number, peer):
        return pltpu.make_async_remote_copy(
            src_ref=src, dst_ref=src, send_sem=spread_send.at[p, number], recv_sem=spread_recv.at[p, number],
            device_id=peer, device_id_type=MESH)

    def z_block(p, j):
        return buf.at[pl.ds(2 * p, 2), xh, zk(1, -j), y, FIRST]

    def z_near(p, j):
        return spread(z_block(p, 0), p, 2 + j if j < 0 else 1 + j, (at(xh, zk(1, -j), y), rows))

    def z_third(p, d):
        return spread(z_block(p, -2 * d), p, 4 if d == 1 else 5, (at(xh, zk(1, -d), y), rows))

    def z_fourth(p, d):
        src = buf.at[2 * p + (0 if d == 1 else 1), xh, zk(1, 2 * d), y, FIRST]
        return spread(src, p, 6 if d == 1 else 7, (at(xh, zk(1, -2 * d), y), rows))

    def z_across(p, j):
        return spread(z_block(p, j), p, 8 + j % NZ, x_peer)

    def y_near(p, j):
        return spread(buf.at[pl.ds(2 * p, 2), xh, z, y, SECOND], p, 15 + j, (at(xh, z, (y + j) % NY), rows))

    def y_across(p):
        return spread(buf.at[pl.ds(2 * p, 2), xh, z, :, SECOND], p, 19, x_peer)

    def spread_begin(p):
        for j in (1, 2, 3):
            y_near(p, j).start()
        for j in (1, -1, 2, -2):
            z_near(p, j).start()
        z_across(p, 0).start()

    def spread_y(p):
        for j in (1, 2, 3):
            y_near(p, j).wait_recv()
        y_across(p).start()

    def spread_z(p):
        for d in (1, -1):
            z_near(p, 2 * d).wait_recv()
            z_third(p, d).start()
            z_fourth(p, d).start()
            z_across(p, -2 * d).start()
        for d in (1, -1):
            z_near(p, d).wait_recv()
            z_across(p, -d).start()

    def spread_far(p):
        for d in (1, -1):
            z_third(p, d).wait_recv()
            z_across(p, -3 * d).start()
        for d in (1, -1):
            z_fourth(p, d).wait_recv()
        z_across(p, 4).start()

    def spread_z_ready(p):
        for j in (0, -2, 2, -1, 1, -3, 3, 4):
            z_across(p, j).wait_recv()

    def spread_drain(p):
        for d in (1, -1):
            for copy in (z_near(p, d), z_near(p, 2 * d), z_third(p, d), z_fourth(p, d)):
                copy.wait_send()
        for j in range(NZ):
            z_across(p, j - 3).wait_send()
        for j in (1, 2, 3):
            y_near(p, j).wait_send()
        y_across(p).wait_send()

    def lanes(d, whole):
        return slice(None) if whole else (0 if d == 1 else 1)

    def begin_z(c, d, part):
        ref = buf.at[c, own if part == 0 else other, z, :, SECOND]
        return remote(ref, ref, c, SEM_B2 + (0 if d == 1 else 5) + part, z_peer[d])

    def begin_y(c, d, part):
        ref = buf.at[c, own if part == 0 else other, :, y, FIRST]
        return remote(ref, ref, c, SEM_A2 + (0 if d == 1 else 3) + part, y_peer[d])

    def gather_z(c, d, k):
        ref = buf.at[c, lanes(d, k < 3), zk(d, k), :, SECOND]
        return remote(ref, ref, c, SEM_B2 + (0 if d == 1 else 5) + k + 1, z_peer[d])

    def gather_y(c, d, k):
        ref = buf.at[c, lanes(d, False), :, yk(d, k), FIRST]
        return remote(ref, ref, c, SEM_A2 + (0 if d == 1 else 3) + k + 1, y_peer[d])

    def both(make, c, k, action):
        for d in (1, -1):
            if k == 0:
                begin = begin_z if make is gather_z else begin_y
                for part in range(2):
                    getattr(begin(c, d, part), action)()
            else:
                getattr(make(c, d, k), action)()

    def begin(make, c, part):
        for d in (1, -1):
            make(c, d, part).start()

    def rows_of(n):
        return n // 4, pl.ds((n % 4) * 2, 2)

    def rotate(c, half):
        high, low = split_terms(buf[c, half].reshape(ROWS // 2, GROUP))
        if c == GROUPS - 1:
            here = slice(half * (ROWS // 2), (half + 1) * (ROWS // 2))
            terms[0, here, :] = high
            terms[1, here, :] = low
        part = grad[:, half * (ROWS // 2):(half + 1) * (ROWS // 2)]
        total = jnp.dot(part, high, preferred_element_type=jnp.float32)
        total += jnp.dot(part, low, preferred_element_type=jnp.float32)
        if half == 0:
            rotated[...] = total
        else:
            partial[c] = (rotated[...] + total).T.reshape(2, 2, QUARTER, COLS)

    def rotate_back(c):
        a_high, a_low = split_terms(adjusted[c].reshape(GROUP, COLS).T)

        def body(n, _):
            xn, zn = rows_of(n)
            high, low = split_terms(buf[c, xn, zn].reshape(256, GROUP))
            here = pl.ds(pl.multiple_of(n * 256, 256), 256)
            update[:, here] += back_product(a_high, a_low, high, low)
            return 0
        lax.fori_loop(0, ROWS // 256, body, 0)

    def rs1_copy(c):
        return remote(partial.at[c, :, 1 - core], rs1.at[c], c, SEM_RS1, core_peer)

    def half_rows(i):
        return pl.ds(i * (QUARTER // 2), QUARTER // 2)

    def rs2_copy(c, i):
        return remote(xsend.at[c, half_rows(i)], rs2.at[c, half_rows(i)], c, SEM_RS2 + i, chip_peer)

    def ax_copy(c, i):
        ref = adjusted.at[c, xlo, core, half_rows(i)]
        return remote(ref, ref, c, SEM_AX + i, chip_peer)

    def ac_copy(c, i):
        ref = adjusted.at[c, xlo, core, half_rows(i)]
        return remote(ref, ref, c, SEM_AC + i, core_peer)

    def af_copy(c, i):
        ref = adjusted.at[c, 1 - xlo, core, half_rows(i)]
        return remote(ref, ref, c, SEM_AF + i, core_peer)

    def moments(c, i):
        part = half_rows(i)
        mine = partial[c, xlo, core, part] + rs1[c, xlo, part] + rs2[c, part]
        one = beta_one * first_in[c, part] + (1.0 - beta_one) * mine
        two = beta_two * second_in[c, part] + (1.0 - beta_two) * mine * mine
        first_out[c, part] = one
        second_out[c, part] = two
        adjusted[c, xlo, core, part] = one / correct_one / (jnp.sqrt(two / correct_two) + epsilon)

    def z_step(c, k):
        if k > 0:
            both(gather_z, c, k - 1, "wait_recv")
        both(gather_z, c, k, "start")

    def y_step(c, k):
        if k > 0:
            both(gather_y, c, k - 1, "wait_recv")
        both(gather_y, c, k, "start")

    def arrive(c):
        both(gather_z, c, 3, "wait_recv")
        both(gather_y, c, 1, "wait_recv")
        rotate(c, 0)
        rotate(c, 1)
        rs1_copy(c).start()

    def cross(c):
        rs1_copy(c).wait_recv()
        for i in range(2):
            part = half_rows(i)
            xsend[c, part] = partial[c, 1 - xlo, core, part] + rs1[c, 1 - xlo, part]
            rs2_copy(c, i).start()

    def adjust(c):
        for i in range(2):
            rs2_copy(c, i).wait_recv()
            moments(c, i)
            ax_copy(c, i).start()
            ac_copy(c, i).start()

    def forward(c):
        for i in range(2):
            ax_copy(c, i).wait_recv()
            af_copy(c, i).start()

    def adjusted_ready(c):
        for i in range(2):
            ac_copy(c, i).wait_recv()
            af_copy(c, i).wait_recv()

    def back(c):
        adjusted_ready(c)
        rotate_back(c)

    spread_begin(0)
    spread_y(0)
    begin(begin_z, 0, 0)
    spread_z(0)
    spread_begin(1)
    begin(begin_z, 1, 0)
    spread_far(0)
    begin(begin_y, 0, 0)
    y_across(0).wait_recv()
    begin(begin_z, 0, 1)
    begin(begin_y, 1, 0)
    begin(begin_z, 1, 1)
    spread_y(1)
    spread_z_ready(0)
    begin(begin_y, 0, 1)
    begin(begin_y, 1, 1)

    spread_z(1)
    z_step(0, 1)
    spread_far(1)
    z_step(1, 1)
    y_across(1).wait_recv()
    z_step(0, 2)
    z_step(2, 0)
    y_step(0, 1)
    z_step(0, 3)
    z_step(1, 2)
    spread_z_ready(1)
    y_step(2, 0)
    z_step(2, 1)
    y_step(1, 1)
    y_step(3, 0)
    z_step(1, 3)
    z_step(3, 0)
    grad_copy.wait()
    prior_copy.wait()
    first_copy.wait()
    second_copy.wait()
    arrive(0)
    z_step(2, 2)
    cross(0)
    z_step(3, 1)
    y_step(2, 1)
    arrive(1)
    adjust(0)
    z_step(2, 3)
    y_step(3, 1)
    cross(1)
    z_step(3, 2)
    forward(0)
    arrive(2)
    z_step(3, 3)
    adjust(1)
    cross(2)
    back(0)
    forward(1)
    arrive(3)
    terms_copy.start()
    adjust(2)
    cross(3)
    back(1)
    forward(2)
    adjust(3)
    back(2)
    update_copy.start()
    forward(3)
    adjusted_ready(3)
    adjusted_out[...] = adjusted[3]
    terms_copy.wait()
    update_copy.wait()

    dealt.wait_send()
    for p in range(2):
        spread_drain(p)

    for c in range(GROUPS):
        for k in range(4):
            both(gather_z, c, k, "wait_send")
        for k in range(2):
            both(gather_y, c, k, "wait_send")
        rs1_copy(c).wait_send()
        for copy in (rs2_copy, ax_copy, ac_copy, af_copy):
            for i in range(2):
                copy(c, i).wait_send()


def finish_kernel(first_in, second_in, adjusted, update, terms, first_out, second_out, update_out, result, sem):
    copies = [pltpu.make_async_copy(first_in, first_out, sem.at[ROWS // 256]),
              pltpu.make_async_copy(second_in, second_out, sem.at[ROWS // 256 + 1])]
    for copy in copies:
        copy.start()
    a_high, a_low = split_terms(adjusted[...].reshape(GROUP, COLS).T)
    for n in range(ROWS // 256):
        here = slice(n * 256, (n + 1) * 256)
        result[:, here] = update[:, here] + back_product(a_high, a_low, terms[0, here, :], terms[1, here, :])
        copies.append(pltpu.make_async_copy(result.at[:, here], update_out.at[:, here], sem.at[n]))
        copies[-1].start()
    for copy in copies:
        copy.wait()


def step(gradient, eigenbasis, first_moment, second_moment, prior_update, group_ids):
    pieces = eigenbasis.reshape(SPREAD, PIECE, 128)
    vmem = pl.BlockSpec(memory_space=pltpu.VMEM)
    hbm = pl.BlockSpec(memory_space=pl.ANY)
    block = (GROUPS, QUARTER, COLS)
    passed = pl.pallas_call(
        kernel,
        out_shape=(
            jax.ShapeDtypeStruct(block, jnp.float32),
            jax.ShapeDtypeStruct(block, jnp.float32),
            jax.ShapeDtypeStruct((2, 2, QUARTER, COLS), jnp.float32),
            jax.ShapeDtypeStruct((COLS, ROWS), jnp.float32),
            jax.ShapeDtypeStruct((2, ROWS, GROUP), jnp.bfloat16),
        ),
        in_specs=[pl.BlockSpec(memory_space=pltpu.SMEM), hbm, hbm, hbm, hbm, hbm],
        out_specs=(vmem, vmem, vmem, hbm, hbm),
        scratch_shapes=[
            pltpu.VMEM((SPREAD, PIECE, 128), jnp.float32),
            pltpu.VMEM((GROUPS, NX, NZ, NY, PIECE, GROUP), jnp.float32),
            pltpu.VMEM((COLS, ROWS), jnp.bfloat16),
            pltpu.VMEM((COLS, GROUP), jnp.float32),
            pltpu.VMEM((GROUPS, 2, 2, QUARTER, COLS), jnp.float32),
            pltpu.VMEM((GROUPS, 2, QUARTER, COLS), jnp.float32),
            pltpu.VMEM(block, jnp.float32),
            pltpu.VMEM(block, jnp.float32),
            pltpu.VMEM((GROUPS, 2, 2, QUARTER, COLS), jnp.float32),
            pltpu.SemaphoreType.DMA((GROUPS, SEMS)),
            pltpu.SemaphoreType.DMA((GROUPS, SEMS)),
            pltpu.SemaphoreType.DMA((7,)),
            pltpu.SemaphoreType.DMA,
            pltpu.SemaphoreType.DMA,
            pltpu.SemaphoreType.DMA((2, 20)),
            pltpu.SemaphoreType.DMA((2, 20)),
            pltpu.VMEM(block, jnp.float32),
            pltpu.VMEM(block, jnp.float32),
            pltpu.SemaphoreType.REGULAR((2,)),
            pltpu.VMEM((COLS, ROWS), jnp.float32),
            pltpu.VMEM((2, ROWS, GROUP), jnp.bfloat16),
        ],
        compiler_params=pltpu.CompilerParams(
            collective_id=0, has_side_effects=True, vmem_limit_bytes=52 * 1024 * 1024),
        cost_estimate=pl.CostEstimate(flops=9_400_000_000, bytes_accessed=14_000_000, transcendentals=0),
    )(group_ids, pieces, first_moment, second_moment, gradient.T, prior_update.T)
    first_out, second_out, update = pl.pallas_call(
        finish_kernel,
        out_shape=(
            jax.ShapeDtypeStruct(block, jnp.float32),
            jax.ShapeDtypeStruct(block, jnp.float32),
            jax.ShapeDtypeStruct((COLS, ROWS), jnp.float32),
        ),
        in_specs=[vmem] * 5,
        out_specs=(hbm,) * 3,
        scratch_shapes=[pltpu.VMEM((COLS, ROWS), jnp.float32), pltpu.SemaphoreType.DMA((ROWS // 256 + 2,))],
        compiler_params=pltpu.CompilerParams(vmem_limit_bytes=24 * 1024 * 1024),
        cost_estimate=pl.CostEstimate(flops=1_400_000_000, bytes_accessed=5_000_000, transcendentals=0),
    )(*passed)
    return first_out, second_out, update.T


def solution(mesh):
    split = P("rows", "cols")
    moment = P(None, "rows", "cols")
    return jax.shard_map(
        step, mesh=mesh,
        in_specs=(split, split, moment, moment, split, P(None)),
        out_specs=(moment, moment, split),
        check_vma=False,
    )
```

```python
import functools

import jax
import jax.numpy as jnp
from jax import lax
from jax.experimental import pallas as pl
from jax.experimental.pallas import tpu as pltpu
from jax.sharding import PartitionSpec as P

MESH = pl.DeviceIdType.MESH

GROUPS = 4
NX, NZ, NY = 2, 8, 4
SPREAD = NX * NZ * NY
PIECE = 32
GROUP = 256
QUARTER = 64
COLS = 448
ROWS = 2048

beta_one = 0.9
beta_two = 0.95
correct_one = 1.0 - 0.9**10
correct_two = 1.0 - 0.95**10
epsilon = 1e-08

BATCHES = ((0, 2, 16), (2, 1, 24), (3, 1, 16))
SLOTS = [pl.ds(begin, count) for begin, count, _ in BATCHES]
FIRST = [pl.ds(0, cut) for _, _, cut in BATCHES]
SECOND = [pl.ds(cut, PIECE - cut) for _, _, cut in BATCHES]
SHARED = [(pl.ds(0, 8), pl.ds(8, cut - 8)) for _, _, cut in BATCHES]
BATCH_OF = (0, 0, 1, 2)

SEM_A2 = 0
SEM_B2 = SEM_A2 + 6
SEM_RS1 = SEM_B2 + 10
SEM_RS2 = SEM_RS1 + 1
SEM_AX = SEM_RS2 + 2
SEM_AC = SEM_AX + 2
SEM_AF = SEM_AC + 2
SEMS = SEM_AF + 2


def split_terms(value):
    high = value.astype(jnp.bfloat16)
    low = (value - high.astype(jnp.float32)).astype(jnp.bfloat16)
    return high, low


def back_product(a_high, a_low, high, low):
    dims = (((1,), (1,)), ((), ()))
    total = lax.dot_general(a_low, high, dims, preferred_element_type=jnp.float32)
    total += lax.dot_general(a_high, low, dims, preferred_element_type=jnp.float32)
    return total + lax.dot_general(a_high, high, dims, preferred_element_type=jnp.float32)


def kernel(ids, basis_hbm, first_hbm, second_hbm, grad_hbm, prior_hbm,
           first_out, second_out, adjusted_out, update_out, terms_out,
           pieces, buf, grad, rotated, partial, rs1, xsend, rs2, adjusted,
           send_sem, recv_sem, local_sem, deal_send, deal_recv,
           spread_send, spread_recv, first_in, second_in, met, update, terms):
    cols = lax.axis_index("cols")
    rows = lax.axis_index("rows")
    xh = cols // (NZ * NY)
    z = (cols // NY) % NZ
    y = cols % NY
    xlo = rows // 2
    core = rows % 2
    sign = 1 - 2 * core

    def at(xh_, z_, y_):
        return (xh_ * NZ + z_) * NY + y_

    own, other = xh, 1 - xh
    x_peer = (at(1 - xh, z, y), rows)
    z_peer = {d: (at(xh, (z + d * sign + NZ) % NZ, y), rows) for d in (1, -1)}
    y_peer = {d: (at(xh, z, (y + d * sign + NY) % NY), rows) for d in (1, -1)}
    core_peer = (cols, xlo * 2 + 1 - core)
    chip_peer = (cols, (1 - xlo) * 2 + core)

    update_copy = pltpu.make_async_copy(update, update_out, local_sem.at[5])
    terms_copy = pltpu.make_async_copy(terms, terms_out, local_sem.at[6])
    grad_copy = pltpu.make_async_copy(grad_hbm, grad, local_sem.at[0])
    prior_copy = pltpu.make_async_copy(prior_hbm, update, local_sem.at[1])
    first_copy = pltpu.make_async_copy(first_hbm, first_in, local_sem.at[3])
    second_copy = pltpu.make_async_copy(second_hbm, second_in, local_sem.at[4])

    def place(j, k, l):
        return (((xh + j) % NX) * NZ + (z + k) % NZ) * NY + (y + l) % NY

    def deal(j, k, l):
        to = place(j, k, l)
        pltpu.make_async_remote_copy(
            src_ref=basis_hbm.at[to], dst_ref=pieces.at[cols], send_sem=deal_send, recv_sem=deal_recv,
            device_id=(to, rows), device_id_type=MESH).start()

    line = [(0, k, 0) for k in range(1, NZ)] + [(0, 0, l) for l in range(1, NY)] + [(1, 0, 0)]
    barrier = pltpu.get_barrier_semaphore()
    for offsets in line:
        pl.semaphore_signal(barrier, inc=1, device_id=(place(*offsets), rows), device_id_type=MESH)
    for peer in (core_peer, chip_peer):
        pl.semaphore_signal(barrier, inc=1, device_id=peer, device_id_type=MESH)
    pl.semaphore_wait(barrier, len(line) + 2)
    for l in range(1, NY):
        pl.semaphore_signal(met.at[0], inc=1, device_id=(place(0, 0, l), rows), device_id_type=MESH)
    for offsets in line:
        deal(*offsets)
    pl.semaphore_wait(met.at[0], NY - 1)
    pl.semaphore_signal(met.at[1], inc=1, device_id=x_peer, device_id_type=MESH)
    for k in range(1, NZ):
        for l in range(1, NY):
            deal(0, k, l)
    pl.semaphore_wait(met.at[1], 1)
    for k in range(NZ):
        for l in range(NY):
            if (k, l) != (0, 0):
                deal(1, k, l)
    own_piece = pltpu.make_async_copy(basis_hbm.at[cols], pieces.at[cols], local_sem.at[2])
    own_piece.start()
    grad_copy.start()
    prior_copy.start()
    first_copy.start()
    second_copy.start()
    own_piece.wait()
    others = pl.ds(0, SPREAD - 1)
    dealt = pltpu.make_async_remote_copy(
        src_ref=basis_hbm.at[others], dst_ref=pieces.at[others], send_sem=deal_send, recv_sem=deal_recv,
        device_id=((cols + 1) % SPREAD, rows), device_id_type=MESH)
    dealt.wait_recv()

    for c in range(GROUPS):
        for half in range(2):
            buf[c, xh, z, y, :, half * 128:(half + 1) * 128] = pieces[ids[c] * 2 + half]

    def remote(src, dst, c, number, peer):
        return pltpu.make_async_remote_copy(
            src_ref=src, dst_ref=dst, send_sem=send_sem.at[c, number], recv_sem=recv_sem.at[c, number],
            device_id=peer, device_id_type=MESH)

    def zk(d, k):
        return (z - d * sign * k + NZ) % NZ

    def yk(d, k):
        return (y - d * sign * k + 2 * NY) % NY

    def spread(src, p, number, peer):
        return pltpu.make_async_remote_copy(
            src_ref=src, dst_ref=src, send_sem=spread_send.at[p, number], recv_sem=spread_recv.at[p, number],
            device_id=peer, device_id_type=MESH)

    def z_block(p, j):
        return buf.at[SLOTS[p], xh, zk(1, -j), y, FIRST[p]]

    def z_near(p, j):
        return spread(z_block(p, 0), p, 2 + j if j < 0 else 1 + j, (at(xh, zk(1, -j), y), rows))

    def z_third(p, d):
        return spread(z_block(p, -2 * d), p, 4 if d == 1 else 5, (at(xh, zk(1, -d), y), rows))

    def z_fourth(p, d):
        src = buf.at[SLOTS[p], xh, zk(1, 2 * d), y, SHARED[p][0 if d == 1 else 1]]
        return spread(src, p, 6 if d == 1 else 7, (at(xh, zk(1, -2 * d), y), rows))

    def z_across(p, j):
        return spread(z_block(p, j), p, 8 + j % NZ, x_peer)

    def y_near(p, j):
        return spread(buf.at[SLOTS[p], xh, z, y, SECOND[p]], p, 15 + j, (at(xh, z, (y + j) % NY), rows))

    def y_across(p):
        return spread(buf.at[SLOTS[p], xh, z, :, SECOND[p]], p, 19, x_peer)

    def spread_begin(p):
        for j in (1, 2, 3):
            y_near(p, j).start()
        for j in (1, -1, 2, -2):
            z_near(p, j).start()
        z_across(p, 0).start()

    def spread_y(p):
        for j in (1, 2, 3):
            y_near(p, j).wait_recv()
        y_across(p).start()

    def spread_z(p):
        for d in (1, -1):
            z_near(p, 2 * d).wait_recv()
            z_third(p, d).start()
            z_fourth(p, d).start()
            z_across(p, -2 * d).start()
        for d in (1, -1):
            z_near(p, d).wait_recv()
            z_across(p, -d).start()

    def spread_far(p):
        for d in (1, -1):
            z_third(p, d).wait_recv()
            z_across(p, -3 * d).start()
        for d in (1, -1):
            z_fourth(p, d).wait_recv()
        z_across(p, 4).start()

    def spread_z_ready(p):
        for j in (0, -2, 2, -1, 1, -3, 3, 4):
            z_across(p, j).wait_recv()

    def spread_drain(p):
        for d in (1, -1):
            for copy in (z_near(p, d), z_near(p, 2 * d), z_third(p, d), z_fourth(p, d)):
                copy.wait_send()
        for j in range(NZ):
            z_across(p, j - 3).wait_send()
        for j in (1, 2, 3):
            y_near(p, j).wait_send()
        y_across(p).wait_send()

    def lanes(d, whole):
        return slice(None) if whole else (0 if d == 1 else 1)

    def begin_z(c, d, part):
        ref = buf.at[c, own if part == 0 else other, z, :, SECOND[BATCH_OF[c]]]
        return remote(ref, ref, c, SEM_B2 + (0 if d == 1 else 5) + part, z_peer[d])

    def begin_y(c, d, part):
        ref = buf.at[c, own if part == 0 else other, :, y, FIRST[BATCH_OF[c]]]
        return remote(ref, ref, c, SEM_A2 + (0 if d == 1 else 3) + part, y_peer[d])

    def gather_z(c, d, k):
        ref = buf.at[c, lanes(d, k < 3), zk(d, k), :, SECOND[BATCH_OF[c]]]
        return remote(ref, ref, c, SEM_B2 + (0 if d == 1 else 5) + k + 1, z_peer[d])

    def gather_y(c, d, k):
        ref = buf.at[c, lanes(d, False), :, yk(d, k), FIRST[BATCH_OF[c]]]
        return remote(ref, ref, c, SEM_A2 + (0 if d == 1 else 3) + k + 1, y_peer[d])

    def both(make, c, k, action):
        for d in (1, -1):
            if k == 0:
                begin = begin_z if make is gather_z else begin_y
                for part in range(2):
                    getattr(begin(c, d, part), action)()
            else:
                getattr(make(c, d, k), action)()

    def begin(make, c, part):
        for d in (1, -1):
            make(c, d, part).start()

    def rows_of(n):
        return n // 4, pl.ds((n % 4) * 2, 2)

    def rotate(c, half):
        high, low = split_terms(buf[c, half].reshape(ROWS // 2, GROUP))
        if c == GROUPS - 1:
            here = slice(half * (ROWS // 2), (half + 1) * (ROWS // 2))
            terms[0, here, :] = high
            terms[1, here, :] = low
        part = grad[:, half * (ROWS // 2):(half + 1) * (ROWS // 2)]
        total = jnp.dot(part, high, preferred_element_type=jnp.float32)
        total += jnp.dot(part, low, preferred_element_type=jnp.float32)
        if half == 0:
            rotated[...] = total
        else:
            partial[c] = (rotated[...] + total).T.reshape(2, 2, QUARTER, COLS)

    def rotate_back(c):
        a_high, a_low = split_terms(adjusted[c].reshape(GROUP, COLS).T)

        def body(n, _):
            xn, zn = rows_of(n)
            high, low = split_terms(buf[c, xn, zn].reshape(256, GROUP))
            here = pl.ds(pl.multiple_of(n * 256, 256), 256)
            update[:, here] += back_product(a_high, a_low, high, low)
            return 0
        lax.fori_loop(0, ROWS // 256, body, 0)

    def rs1_copy(c):
        return remote(partial.at[c, :, 1 - core], rs1.at[c], c, SEM_RS1, core_peer)

    def half_rows(i):
        return pl.ds(i * (QUARTER // 2), QUARTER // 2)

    def rs2_copy(c, i):
        return remote(xsend.at[c, half_rows(i)], rs2.at[c, half_rows(i)], c, SEM_RS2 + i, chip_peer)

    def ax_copy(c, i):
        ref = adjusted.at[c, xlo, core, half_rows(i)]
        return remote(ref, ref, c, SEM_AX + i, chip_peer)

    def ac_copy(c, i):
        ref = adjusted.at[c, xlo, core, half_rows(i)]
        return remote(ref, ref, c, SEM_AC + i, core_peer)

    def af_copy(c, i):
        ref = adjusted.at[c, 1 - xlo, core, half_rows(i)]
        return remote(ref, ref, c, SEM_AF + i, core_peer)

    def moments(c, i):
        part = half_rows(i)
        mine = partial[c, xlo, core, part] + rs1[c, xlo, part] + rs2[c, part]
        one = beta_one * first_in[c, part] + (1.0 - beta_one) * mine
        two = beta_two * second_in[c, part] + (1.0 - beta_two) * mine * mine
        first_out[c, part] = one
        second_out[c, part] = two
        adjusted[c, xlo, core, part] = one / correct_one / (jnp.sqrt(two / correct_two) + epsilon)

    def z_step(c, k):
        if k > 0:
            both(gather_z, c, k - 1, "wait_recv")
        both(gather_z, c, k, "start")

    def y_step(c, k):
        if k > 0:
            both(gather_y, c, k - 1, "wait_recv")
        both(gather_y, c, k, "start")

    def arrive(c):
        both(gather_z, c, 3, "wait_recv")
        both(gather_y, c, 1, "wait_recv")
        rotate(c, 0)
        rotate(c, 1)
        rs1_copy(c).start()

    def cross(c):
        rs1_copy(c).wait_recv()
        for i in range(2):
            part = half_rows(i)
            xsend[c, part] = partial[c, 1 - xlo, core, part] + rs1[c, 1 - xlo, part]
            rs2_copy(c, i).start()

    def adjust(c):
        for i in range(2):
            rs2_copy(c, i).wait_recv()
            moments(c, i)
            ax_copy(c, i).start()
            ac_copy(c, i).start()

    def forward(c):
        for i in range(2):
            ax_copy(c, i).wait_recv()
            af_copy(c, i).start()

    def adjusted_ready(c):
        for i in range(2):
            ac_copy(c, i).wait_recv()
            af_copy(c, i).wait_recv()

    def back(c):
        adjusted_ready(c)
        rotate_back(c)

    spread_begin(0)
    spread_y(0)
    begin(begin_z, 0, 0)
    spread_z(0)
    spread_begin(1)
    begin(begin_z, 1, 0)
    spread_far(0)
    begin(begin_y, 0, 0)
    y_across(0).wait_recv()
    begin(begin_z, 0, 1)
    begin(begin_y, 1, 0)
    begin(begin_z, 1, 1)
    spread_begin(2)
    spread_y(1)
    spread_z_ready(0)
    begin(begin_y, 0, 1)
    begin(begin_y, 1, 1)

    spread_y(2)
    spread_z(1)
    z_step(0, 1)
    spread_z(2)
    spread_far(1)
    z_step(1, 1)
    y_across(1).wait_recv()
    z_step(0, 2)
    z_step(2, 0)
    y_step(0, 1)
    spread_far(2)
    z_step(0, 3)
    z_step(1, 2)
    spread_z_ready(1)
    y_step(2, 0)
    z_step(2, 1)
    y_step(1, 1)
    spread_z_ready(2)
    y_step(3, 0)
    z_step(1, 3)
    y_across(2).wait_recv()
    z_step(3, 0)
    grad_copy.wait()
    prior_copy.wait()
    first_copy.wait()
    second_copy.wait()
    arrive(0)
    z_step(2, 2)
    cross(0)
    z_step(3, 1)
    y_step(2, 1)
    arrive(1)
    adjust(0)
    z_step(2, 3)
    y_step(3, 1)
    cross(1)
    z_step(3, 2)
    forward(0)
    arrive(2)
    z_step(3, 3)
    adjust(1)
    cross(2)
    back(0)
    forward(1)
    arrive(3)
    terms_copy.start()
    adjust(2)
    cross(3)
    back(1)
    forward(2)
    adjust(3)
    back(2)
    update_copy.start()
    forward(3)
    adjusted_ready(3)
    adjusted_out[...] = adjusted[3]
    terms_copy.wait()
    update_copy.wait()

    dealt.wait_send()
    for p in range(len(BATCHES)):
        spread_drain(p)

    for c in range(GROUPS):
        for k in range(4):
            both(gather_z, c, k, "wait_send")
        for k in range(2):
            both(gather_y, c, k, "wait_send")
        rs1_copy(c).wait_send()
        for copy in (rs2_copy, ax_copy, ac_copy, af_copy):
            for i in range(2):
                copy(c, i).wait_send()


def finish_kernel(first_in, second_in, adjusted, update, terms, first_out, second_out, update_out, result, sem):
    copies = [pltpu.make_async_copy(first_in, first_out, sem.at[ROWS // 256]),
              pltpu.make_async_copy(second_in, second_out, sem.at[ROWS // 256 + 1])]
    for copy in copies:
        copy.start()
    a_high, a_low = split_terms(adjusted[...].reshape(GROUP, COLS).T)
    for n in range(ROWS // 256):
        here = slice(n * 256, (n + 1) * 256)
        result[:, here] = update[:, here] + back_product(a_high, a_low, terms[0, here, :], terms[1, here, :])
        copies.append(pltpu.make_async_copy(result.at[:, here], update_out.at[:, here], sem.at[n]))
        copies[-1].start()
    for copy in copies:
        copy.wait()


def step(gradient, eigenbasis, first_moment, second_moment, prior_update, group_ids):
    pieces = eigenbasis.reshape(SPREAD, PIECE, 128)
    vmem = pl.BlockSpec(memory_space=pltpu.VMEM)
    hbm = pl.BlockSpec(memory_space=pl.ANY)
    block = (GROUPS, QUARTER, COLS)
    passed = pl.pallas_call(
        kernel,
        out_shape=(
            jax.ShapeDtypeStruct(block, jnp.float32),
            jax.ShapeDtypeStruct(block, jnp.float32),
            jax.ShapeDtypeStruct((2, 2, QUARTER, COLS), jnp.float32),
            jax.ShapeDtypeStruct((COLS, ROWS), jnp.float32),
            jax.ShapeDtypeStruct((2, ROWS, GROUP), jnp.bfloat16),
        ),
        in_specs=[pl.BlockSpec(memory_space=pltpu.SMEM), hbm, hbm, hbm, hbm, hbm],
        out_specs=(vmem, vmem, vmem, hbm, hbm),
        scratch_shapes=[
            pltpu.VMEM((SPREAD, PIECE, 128), jnp.float32),
            pltpu.VMEM((GROUPS, NX, NZ, NY, PIECE, GROUP), jnp.float32),
            pltpu.VMEM((COLS, ROWS), jnp.bfloat16),
            pltpu.VMEM((COLS, GROUP), jnp.float32),
            pltpu.VMEM((GROUPS, 2, 2, QUARTER, COLS), jnp.float32),
            pltpu.VMEM((GROUPS, 2, QUARTER, COLS), jnp.float32),
            pltpu.VMEM(block, jnp.float32),
            pltpu.VMEM(block, jnp.float32),
            pltpu.VMEM((GROUPS, 2, 2, QUARTER, COLS), jnp.float32),
            pltpu.SemaphoreType.DMA((GROUPS, SEMS)),
            pltpu.SemaphoreType.DMA((GROUPS, SEMS)),
            pltpu.SemaphoreType.DMA((7,)),
            pltpu.SemaphoreType.DMA,
            pltpu.SemaphoreType.DMA,
            pltpu.SemaphoreType.DMA((len(BATCHES), 20)),
            pltpu.SemaphoreType.DMA((len(BATCHES), 20)),
            pltpu.VMEM(block, jnp.float32),
            pltpu.VMEM(block, jnp.float32),
            pltpu.SemaphoreType.REGULAR((2,)),
            pltpu.VMEM((COLS, ROWS), jnp.float32),
            pltpu.VMEM((2, ROWS, GROUP), jnp.bfloat16),
        ],
        compiler_params=pltpu.CompilerParams(
            collective_id=0, has_side_effects=True, vmem_limit_bytes=52 * 1024 * 1024),
        cost_estimate=pl.CostEstimate(flops=9_400_000_000, bytes_accessed=14_000_000, transcendentals=0),
    )(group_ids, pieces, first_moment, second_moment, gradient.T, prior_update.T)
    first_out, second_out, update = pl.pallas_call(
        finish_kernel,
        out_shape=(
            jax.ShapeDtypeStruct(block, jnp.float32),
            jax.ShapeDtypeStruct(block, jnp.float32),
            jax.ShapeDtypeStruct((COLS, ROWS), jnp.float32),
        ),
        in_specs=[vmem] * 5,
        out_specs=(hbm,) * 3,
        scratch_shapes=[pltpu.VMEM((COLS, ROWS), jnp.float32), pltpu.SemaphoreType.DMA((ROWS // 256 + 2,))],
        compiler_params=pltpu.CompilerParams(vmem_limit_bytes=24 * 1024 * 1024),
        cost_estimate=pl.CostEstimate(flops=1_400_000_000, bytes_accessed=5_000_000, transcendentals=0),
    )(*passed)
    return first_out, second_out, update.T


def solution(mesh):
    split = P("rows", "cols")
    moment = P(None, "rows", "cols")
    return jax.shard_map(
        step, mesh=mesh,
        in_specs=(split, split, moment, moment, split, P(None)),
        out_specs=(moment, moment, split),
        check_vma=False,
    )
```
